512 devices in a mesh: inner: 16 (over x_hi, y, core), outer: 32 (over z, x_lo).
Axes of the slice: x: 4 (x_hi: 2, x_lo: 2; x = x_hi * 2 + x_lo), y: 4, z: 16, core: 2. Of those that a mesh axis runs over, the one named last changes fastest.
Arguments:
- query: bfloat16 [65536, 4096], P(('inner', 'outer')), may hold values from -6 to 6
- key: bfloat16 [65536, 512], P(('inner', 'outer')), may hold values from -6 to 6
- value: bfloat16 [65536, 512], P(('inner', 'outer')), may hold values from -6 to 6
- out: bfloat16 [65536, 4096], P(('inner', 'outer')), may hold values from -6 to 6
- dout: bfloat16 [65536, 4096], P(('inner', 'outer')), may hold values from -6 to 6
- lse: float32 [32, 65536], P(None, ('inner', 'outer')), may hold values from 6.5 to 8.5
- segment: int32 [65536], P(('inner', 'outer')), may hold values from 0 to 511, never falling along the last dimension, each value on 1 to 256 neighbouring positions
- bitmap: int32 [512], P(('inner', 'outer')), may hold values from 2 to 65535, as said below
Outputs:
- dquery: bfloat16 [65536, 4096], P(('inner', 'outer'))
- dkey: bfloat16 [65536, 512], P(('inner', 'outer'))
- dvalue: bfloat16 [65536, 512], P(('inner', 'outer'))
The draws below stay inside these ranges and needn't reach their ends.
Inputs may be any that keep to these rules, and one draw needn't show every extreme that they name: `bitmap`: bit 1 of every entry is set: a tile always sees the tile just before it.
All inputs are finite; a program needn't handle non-finite values.
Results may differ from the reference program's by a relative error of at most 0.006.
Values may be sent and summed in bfloat16 or wider, within the bound.
No kernel may reach another device: no remote copies, remote signals or barrier semaphores. Data moves between devices by JAX's collectives and lax.ppermute only.
A program may use at most 128 MiB of HBM per device.

```python
import math
import jax
import jax.numpy as jnp
import numpy as np
from jax import lax

QUERY_HEADS = 32
KEY_VALUE_HEADS = 4
HEAD_SIZE = 128
TOK_DEV = 128
VISIBLE_TILES = 16
NBLK = 512
TOKEN_COUNT = 65536


def draw_bitmap(key, part):
    key = jax.random.fold_in(key, 11)
    words = jax.random.randint(key, (NBLK,), 0, 65536, dtype=jnp.int32)
    return jnp.bitwise_or(words, 2)


def levels(own_key, shape, cuts, low, top_value):
    gain = 1.0
    for axis_at, parts in cuts:
        draws = jax.random.uniform(jax.random.fold_in(jax.random.fold_in(own_key, 6), axis_at), (parts,), jnp.float32, low / len(cuts), top_value / len(cuts))
        gain = gain * jnp.repeat(jnp.exp(draws), shape[axis_at] // parts).reshape((-1,) + (1,) * (len(shape) - 1 - axis_at))
    return gain


def length_profile(count, total, limit, slope):
    loads = [(1 << 20) // math.isqrt(rank ** slope) + 1 for rank in range(2, count + 1)]
    spare, given = total - limit - (count - 1), [1] * (count - 1)
    while spare > 0:
        movable = [i for i in range(count - 1) if given[i] < limit]
        mass, left = sum([loads[i] for i in movable]), spare
        for i in movable:
            extra = min(limit - given[i], max(1, left * loads[i] // mass), spare)
            given[i] = given[i] + extra
            spare = spare - extra
    return np.array([limit] + given)


def uneven(rng, number_of, total, most, lean):
    if number_of == 2:
        one = jax.random.randint(rng, (), max(1, total - most), min(most, total - 1) + 1)
        return jnp.stack([one, total - one])
    tallies = jnp.asarray(length_profile(number_of, total, most, lean), jnp.int32)
    pairs = (number_of - 1) // 2
    source_of, taker = tallies[1:1 + 2 * pairs:2], tallies[2:2 + 2 * pairs:2]
    slack = jnp.minimum(source_of - 1, most - taker)
    shifted = jax.random.randint(jax.random.fold_in(rng, 1), (pairs,), 0, 1 << 20) % (slack + 1)
    tallies = tallies.at[1:1 + 2 * pairs:2].set(source_of - shifted).at[2:2 + 2 * pairs:2].set(taker + shifted)
    return tallies[jax.random.permutation(jax.random.fold_in(rng, 2), number_of)]


def scatter_about(rng, dims, deviation, bound, pieces=(), held_as=jnp.bfloat16):
    drawn = jax.random.normal(rng, dims, jnp.float32) * deviation
    if len(pieces) > 0:
        drawn = levels(rng, dims, pieces, -0.22, 0.18) * drawn
    return jnp.clip(drawn, min=-bound, max=bound).astype(held_as)


def setup_inputs(seed: int = 0) -> dict:
    seeds = jax.random.split(jax.random.key(seed), 9)
    query = scatter_about(seeds[0], (TOKEN_COUNT, QUERY_HEADS * HEAD_SIZE), 1.0, 6.0, ((0, 512),))
    key = scatter_about(seeds[1], (TOKEN_COUNT, KEY_VALUE_HEADS * HEAD_SIZE), 1.0, 6.0, ((0, 512),))
    value = scatter_about(seeds[2], (TOKEN_COUNT, KEY_VALUE_HEADS * HEAD_SIZE), 1.0, 6.0, ((0, 512),))
    out = scatter_about(seeds[3], (TOKEN_COUNT, QUERY_HEADS * HEAD_SIZE), 1.0, 6.0, ((0, 512),))
    dout = scatter_about(seeds[4], (TOKEN_COUNT, QUERY_HEADS * HEAD_SIZE), 1.0, 6.0, ((0, 512),))
    lse = jnp.clip(6.5 + 2.0 * jax.random.uniform(seeds[5], (QUERY_HEADS, TOKEN_COUNT), jnp.float32) ** levels(seeds[5], (QUERY_HEADS, TOKEN_COUNT), ((1, 512),), -0.2, 0.2), 6.5, 8.5)
    segment = jnp.searchsorted(jnp.cumsum(uneven(seeds[6], NBLK, TOKEN_COUNT, 2 * TOK_DEV, 1)), jnp.arange(TOKEN_COUNT), side="right").astype(jnp.int32)
    bitmap = draw_bitmap(jax.random.fold_in(seeds[8], 71), 0)
    return {"query": query, "key": key, "value": value, "out": out, "dout": dout, "lse": lse, "segment": segment, "bitmap": bitmap}


def reference(query, key, value, out, dout, lse, segment, bitmap):
    single_float = jnp.float32
    token_input = query.shape[0]
    group_size = QUERY_HEADS // KEY_VALUE_HEADS
    tile_length = TOK_DEV
    nblk = token_input // tile_length
    padding = (VISIBLE_TILES - 1) * tile_length
    scale = HEAD_SIZE ** -0.5
    delta_rows = jnp.sum((dout.astype(single_float) * out.astype(single_float)).reshape(token_input, QUERY_HEADS, HEAD_SIZE), axis=-1)
    key_padded = jnp.concatenate([jnp.zeros((padding, KEY_VALUE_HEADS * HEAD_SIZE), key.dtype), key], axis=0)
    value_padded = jnp.concatenate([jnp.zeros((padding, KEY_VALUE_HEADS * HEAD_SIZE), value.dtype), value], axis=0)
    seg_pad = jnp.concatenate([jnp.zeros((padding,), jnp.int32), segment.astype(jnp.int32)], axis=0)
    tile_rows = jnp.arange(tile_length, dtype=jnp.int32)
    cols = jnp.arange(VISIBLE_TILES * tile_length, dtype=jnp.int32)
    offset = (VISIBLE_TILES - 1 - cols // tile_length).astype(jnp.int32)

    def step(carry, block):
        key_gradient_total, value_gradient_total = carry
        start_row = (block * tile_length).astype(jnp.int32)
        query_block = lax.dynamic_slice_in_dim(query, start_row, tile_length, 0).astype(single_float).reshape(tile_length, KEY_VALUE_HEADS, group_size, HEAD_SIZE)
        output_gradient_block = lax.dynamic_slice_in_dim(dout, start_row, tile_length, 0).astype(single_float).reshape(tile_length, KEY_VALUE_HEADS, group_size, HEAD_SIZE)
        logsumexp_block = lax.dynamic_slice_in_dim(lse, start_row, tile_length, 1).reshape(KEY_VALUE_HEADS, group_size, tile_length)
        delta_block = lax.dynamic_slice_in_dim(delta_rows, start_row, tile_length, 0).T.reshape(KEY_VALUE_HEADS, group_size, tile_length)
        key_block = lax.dynamic_slice_in_dim(key_padded, start_row, VISIBLE_TILES * tile_length, 0).astype(single_float).reshape(VISIBLE_TILES * tile_length, KEY_VALUE_HEADS, HEAD_SIZE)
        value_block = lax.dynamic_slice_in_dim(value_padded, start_row, VISIBLE_TILES * tile_length, 0).astype(single_float).reshape(VISIBLE_TILES * tile_length, KEY_VALUE_HEADS, HEAD_SIZE)
        q_seg = lax.dynamic_slice_in_dim(segment.astype(jnp.int32), start_row, tile_length, 0)
        k_seg = lax.dynamic_slice_in_dim(seg_pad, start_row, VISIBLE_TILES * tile_length, 0)
        word = bitmap[block]
        live = (jnp.bitwise_and(jnp.right_shift(word, offset), 1) == 1) | (offset == 0)
        valid = block - offset >= 0
        causal = (offset[None, :] > 0) | ((cols % tile_length)[None, :] <= tile_rows[:, None])
        blocked = ((q_seg % 2) == 1)[:, None] & ((k_seg % 2) == 1)[None, :] & (q_seg[:, None] != k_seg[None, :])
        allowed = causal & jnp.logical_not(blocked) & (live & valid)[None, :]
        scores = jnp.einsum('qghd,kgd->ghqk', query_block, key_block) * scale
        prob = jnp.where(allowed[None, None], jnp.exp(scores - logsumexp_block[..., None]), jnp.float32(0.0))
        prob_half = lax.optimization_barrier(prob.astype(jnp.bfloat16)).astype(single_float)
        value_gradient = jnp.einsum('ghqk,qghd->kgd', prob_half, output_gradient_block)
        dprob = jnp.einsum('qghd,kgd->ghqk', output_gradient_block, value_block)
        dscore = lax.optimization_barrier((prob * (dprob - delta_block[..., None])).astype(jnp.bfloat16)).astype(single_float)
        dq = jnp.einsum('ghqk,kgd->qghd', dscore, key_block) * scale
        key_gradient = jnp.einsum('ghqk,qghd->kgd', dscore, query_block) * scale
        previous_key = lax.dynamic_slice_in_dim(key_gradient_total, start_row, VISIBLE_TILES * tile_length, 0)
        previous_value = lax.dynamic_slice_in_dim(value_gradient_total, start_row, VISIBLE_TILES * tile_length, 0)
        key_gradient_total = lax.dynamic_update_slice_in_dim(key_gradient_total, previous_key + key_gradient.reshape(VISIBLE_TILES * tile_length, KEY_VALUE_HEADS * HEAD_SIZE), start_row, 0)
        value_gradient_total = lax.dynamic_update_slice_in_dim(value_gradient_total, previous_value + value_gradient.reshape(VISIBLE_TILES * tile_length, KEY_VALUE_HEADS * HEAD_SIZE), start_row, 0)
        return (key_gradient_total, value_gradient_total), dq.reshape(tile_length, QUERY_HEADS * HEAD_SIZE).astype(jnp.bfloat16)

    empty_block = jnp.zeros((padding + token_input, KEY_VALUE_HEADS * HEAD_SIZE), single_float)
    (dk_all, dv_all), dq_all = lax.scan(step, (empty_block, empty_block), jnp.arange(nblk, dtype=jnp.int32))
    dquery = dq_all.reshape(token_input, QUERY_HEADS * HEAD_SIZE)
    return dquery, dk_all[padding:].astype(jnp.bfloat16), dv_all[padding:].astype(jnp.bfloat16)
```

```python
import functools
import math

import jax
import jax.numpy as jnp
from jax import lax
from jax.experimental import pallas as pl
from jax.experimental.pallas import tpu as pltpu
from jax.sharding import PartitionSpec as P

QUERY_HEADS = 32
KEY_VALUE_HEADS = 4
HEAD_SIZE = 128
VISIBLE_TILES = 16
TILE = 128
GROUP = QUERY_HEADS // KEY_VALUE_HEADS

MY_HEADS = QUERY_HEADS // 2
MY_KV = KEY_VALUE_HEADS // 2
KV_COLS = MY_KV * HEAD_SIZE
Q_COLS = MY_HEADS * HEAD_SIZE
HOPS = VISIBLE_TILES // 2

SEG_ROWS = 16
K1, V1, SEG, K0, V0 = 0, TILE, 2 * TILE, 2 * TILE + SEG_ROWS, 3 * TILE + SEG_ROWS
HALF_ROWS = 2 * TILE + SEG_ROWS
FULL_ROWS = 4 * TILE + SEG_ROWS

SMALL_ROWS = 40
SCALE = HEAD_SIZE**-0.5
LOG2E = math.log2(math.e)
NEVER = -1e30
AXES = ("inner", "outer")


def shift(array, by):
    count = lax.axis_size(AXES)
    pairs = [(i, i + by) for i in range(count) if 0 <= i + by < count]
    return lax.ppermute(array, AXES, pairs)


def swap(array):
    count = lax.axis_size(AXES)
    return lax.ppermute(array, AXES, [(i, i ^ 1) for i in range(count)])


def nt(a, b):
    return lax.dot_general(a, b, (((1,), (1,)), ((), ())), preferred_element_type=jnp.float32)


def nn(a, b):
    return jnp.dot(a, b, preferred_element_type=jnp.float32)


def turn_kernel(column_ref, q_own, do_own, q_par, sm_own, sm_par, q_turned, do_turned, columns):
    column = column_ref[0]

    @pl.loop(0, MY_KV)
    def _(kv):
        first = pl.multiple_of(kv * GROUP, GROUP)
        rows = []
        for at in (first, MY_HEADS + first):
            rows.append(
                jnp.concatenate([sm_own[pl.ds(at, GROUP), :], sm_par[pl.ds(at, GROUP), :]], axis=1)
            )
        rows.append(jnp.zeros((TILE - 2 * GROUP, 2 * TILE), jnp.float32))
        columns[kv] = jnp.concatenate(rows, axis=0).T
        for i in range(GROUP):
            head = first + i
            cols = pl.ds(pl.multiple_of(head * HEAD_SIZE, HEAD_SIZE), HEAD_SIZE)
            own_cols = pl.ds(
                pl.multiple_of((column * MY_HEADS + head) * HEAD_SIZE, HEAD_SIZE), HEAD_SIZE
            )
            at = slice(i * 2 * TILE, (i + 1) * 2 * TILE)
            q_turned[kv, :, at] = jnp.concatenate(
                [q_own[:, own_cols].T, q_par[0:TILE, cols].T], axis=1
            )
            do_turned[kv, :, at] = jnp.concatenate(
                [do_own[:, own_cols].T, q_par[TILE : 2 * TILE, cols].T], axis=1
            )


def turned(column, query, dout, other, sm_own, sm_par):
    here = pl.BlockSpec(memory_space=pltpu.VMEM)
    wide = jax.ShapeDtypeStruct((MY_KV, HEAD_SIZE, GROUP * 2 * TILE), jnp.bfloat16)
    return pl.pallas_call(
        turn_kernel,
        in_specs=[pl.BlockSpec(memory_space=pltpu.SMEM)] + [here] * 5,
        out_specs=[here] * 3,
        out_shape=[wide, wide, jax.ShapeDtypeStruct((MY_KV, 2 * TILE, TILE), jnp.float32)],
        compiler_params=pltpu.CompilerParams(vmem_limit_bytes=16 * 1024 * 1024),
        cost_estimate=pl.CostEstimate(flops=2**20, bytes_accessed=2**23, transcendentals=0),
    )(column[None].astype(jnp.int32), query, dout, other, sm_own, sm_par)


def pair_kernel(offsets, first, last, where_ref, *refs):
    count = len(offsets)
    q_own, q_par, do_own, sm_own, sm_par, q_turned, do_turned, columns = refs[:8]
    blocks = refs[8 : 8 + count]
    at = 8 + count
    dq_in = None
    if not first:
        dq_in = refs[at]
        at += 1
    parts = refs[at : at + count]
    at += count
    if last:
        dq_own, dq_par = refs[at : at + 2]
        at += 2
    else:
        dq_out = refs[at]
        at += 1
    biases = refs[at : at + count]
    column, place = where_ref[0], where_ref[1]

    row = lax.broadcasted_iota(jnp.int32, (TILE, TILE), 0)
    col = lax.broadcasted_iota(jnp.int32, (TILE, TILE), 1)
    for r, small in enumerate((sm_own, sm_par)):
        xq = column if r == 0 else 1 - column
        tile = place - column + xq
        words = small[2 * MY_HEADS + 1 : 2 * MY_HEADS + 2, :].astype(jnp.int32)
        q_seg = jnp.broadcast_to(small[2 * MY_HEADS : 2 * MY_HEADS + 1, :], (TILE, TILE)).T
        for n, s in enumerate(offsets):
            seg = blocks[n][SEG : SEG + SEG_ROWS, :TILE].astype(jnp.float32)
            for t in (1,) if s == HOPS else (0, 1):
                k_seg = jnp.broadcast_to(seg[1 - t : 2 - t, :], (TILE, TILE))
                w = 2 * s + xq - t
                bit = lax.shift_right_logical(words, jnp.broadcast_to(jnp.maximum(w, 0), words.shape)) & 1
                inside = (w >= 0) & (w < VISIBLE_TILES) & (tile - w >= 0)
                bit = jnp.where(w == 0, 1, bit)
                bit = jnp.where(inside, bit, 0)
                seen = (k_seg * q_seg * (k_seg - q_seg) == 0.0) & (
                    jnp.broadcast_to(bit, (TILE, TILE)) == 1
                )
                if s == 0:
                    seen = seen & ((row >= col) | (w != 0))
                k_at = 0 if s == HOPS else t * TILE
                biases[n][r * TILE : (r + 1) * TILE, k_at : k_at + TILE] = jnp.where(
                    seen, 0.0, NEVER
                )

    @pl.loop(0, MY_KV)
    def _(kv):
        kv_cols = pl.ds(pl.multiple_of(kv * HEAD_SIZE, HEAD_SIZE), HEAD_SIZE)
        loaded = []
        for n, s in enumerate(offsets):
            block = blocks[n]
            if s == HOPS:
                k, v = block[K1 : K1 + TILE, kv_cols], block[V1 : V1 + TILE, kv_cols]
            else:
                k = jnp.concatenate(
                    [block[K0 : K0 + TILE, kv_cols], block[K1 : K1 + TILE, kv_cols]], axis=0
                )
                v = jnp.concatenate(
                    [block[V0 : V0 + TILE, kv_cols], block[V1 : V1 + TILE, kv_cols]], axis=0
                )
            loaded.append((k, v, k.T, v.T))
        q_heads, do_heads = [], []
        for i in range(GROUP):
            head = kv * GROUP + i
            cols = pl.ds(pl.multiple_of(head * HEAD_SIZE, HEAD_SIZE), HEAD_SIZE)
            own_cols = pl.ds(
                pl.multiple_of((column * MY_HEADS + head) * HEAD_SIZE, HEAD_SIZE), HEAD_SIZE
            )
            q_heads += [q_own[:, own_cols], q_par[0:TILE, cols]]
            do_heads += [do_own[:, own_cols], q_par[TILE : 2 * TILE, cols]]
        q = jnp.concatenate(q_heads, axis=0)
        do = jnp.concatenate(do_heads, axis=0)
        totals = []
        dq = None
        for n in range(count):
            k, v, k_turned, v_turned = loaded[n]
            scores = nn(q, k_turned)
            dprob = nn(do, v_turned)
            probs, dscores = [], []
            for i in range(GROUP):
                at = slice(i * 2 * TILE, (i + 1) * 2 * TILE)
                neg_lse = columns[kv, :, i : i + 1]
                delta = columns[kv, :, GROUP + i : GROUP + i + 1]
                prob = jnp.exp2(scores[at] * (SCALE * LOG2E) + (biases[n][...] + neg_lse))
                probs.append(prob.astype(jnp.bfloat16))
                dscores.append((prob * (dprob[at] - delta)).astype(jnp.bfloat16))
            prob = jnp.concatenate(probs, axis=0)
            dscore = jnp.concatenate(dscores, axis=0)
            totals.append((nn(q_turned[kv], dscore), nn(do_turned[kv], prob)))
            more = nn(dscore, k)
            dq = more if dq is None else dq + more
        for i in range(GROUP):
            head = kv * GROUP + i
            cols = pl.ds(pl.multiple_of(head * HEAD_SIZE, HEAD_SIZE), HEAD_SIZE)
            part = dq[i * 2 * TILE : (i + 1) * 2 * TILE]
            if not first:
                part = part + dq_in[head]
            if last:
                part = (part * SCALE).astype(jnp.bfloat16)
                dq_own[:, cols] = part[:TILE]
                dq_par[:, cols] = part[TILE:]
            else:
                dq_out[head] = part
        for n, s in enumerate(offsets):
            dk_all = (totals[n][0] * SCALE).T.astype(jnp.bfloat16)
            dv_all = totals[n][1].T.astype(jnp.bfloat16)
            if s == HOPS:
                parts[n][0:TILE, kv_cols] = dk_all
                parts[n][TILE : 2 * TILE, kv_cols] = dv_all
            else:
                parts[n][0:TILE, kv_cols] = dk_all[TILE:]
                parts[n][TILE : 2 * TILE, kv_cols] = dv_all[TILE:]
                parts[n][2 * TILE : 3 * TILE, kv_cols] = dk_all[:TILE]
                parts[n][3 * TILE : 4 * TILE, kv_cols] = dv_all[:TILE]


def pair_grads(offsets, where, query, dout, other, sm_own, sm_par, turns, blocks, dq, last):
    first = dq is None
    keys = [TILE if s == HOPS else 2 * TILE for s in offsets]
    here = pl.BlockSpec(memory_space=pltpu.VMEM)
    args = [query, other, dout, sm_own, sm_par, *turns, *blocks]
    if not first:
        args.append(dq)
    out_shape = [jax.ShapeDtypeStruct((2 * k, KV_COLS), jnp.bfloat16) for k in keys]
    if last:
        out_shape += [jax.ShapeDtypeStruct((TILE, Q_COLS), jnp.bfloat16)] * 2
    else:
        out_shape.append(jax.ShapeDtypeStruct((MY_HEADS, 2 * TILE, HEAD_SIZE), jnp.float32))
    flops = sum(10 * MY_HEADS * k * 2 * TILE * HEAD_SIZE for k in keys)
    return pl.pallas_call(
        functools.partial(pair_kernel, offsets, first, last),
        in_specs=[pl.BlockSpec(memory_space=pltpu.SMEM)] + [here] * len(args),
        out_specs=[here] * len(out_shape),
        out_shape=out_shape,
        scratch_shapes=[pltpu.VMEM((2 * TILE, k), jnp.float32) for k in keys],
        input_output_aliases={} if first or last else {len(args): len(out_shape) - 1},
        compiler_params=pltpu.CompilerParams(vmem_limit_bytes=24 * 1024 * 1024),
        cost_estimate=pl.CostEstimate(
            flops=flops,
            bytes_accessed=8 * 1024 * 1024,
            transcendentals=sum(MY_HEADS * k * 2 * TILE for k in keys),
        ),
    )(where, *args)


def add_back(arrived, part):
    if arrived.shape[0] < part.shape[0]:
        arrived = jnp.pad(arrived, ((0, part.shape[0] - arrived.shape[0]), (0, 0)))
    return (arrived.astype(jnp.float32) + part.astype(jnp.float32)).astype(jnp.bfloat16)


def row_kernel(column_ref, out_ref, dout_ref, lse_ref, tail_ref, own_ref, other_ref):
    step = pl.program_id(0)
    heads = QUERY_HEADS // 2
    ones = jnp.ones((8, HEAD_SIZE), jnp.bfloat16)
    rows = []
    for i in range(heads):
        cols = slice(i * HEAD_SIZE, (i + 1) * HEAD_SIZE)
        product = out_ref[:, cols].astype(jnp.float32) * dout_ref[:, cols].astype(jnp.float32)
        high = product.astype(jnp.bfloat16)
        low = (product - high.astype(jnp.float32)).astype(jnp.bfloat16)
        rows.append((nt(ones, high) + nt(ones, low))[:1])
    delta = jnp.concatenate(rows, axis=0)

    def fill(ref):
        ref[0:heads, :] = lse_ref[...] * (-LOG2E)
        ref[heads : 2 * heads, :] = delta
        ref[2 * heads : SMALL_ROWS, :] = tail_ref[...]

    @pl.when(step == column_ref[0])
    def _():
        fill(own_ref)

    @pl.when(step != column_ref[0])
    def _():
        fill(other_ref)


def row_values(column, out, dout, lse, seg_code, bitmap):
    tail = jnp.concatenate(
        [
            seg_code.astype(jnp.float32)[None, :],
            jnp.broadcast_to(bitmap.astype(jnp.float32)[None, :], (1, TILE)),
            jnp.zeros((SMALL_ROWS - 2 * MY_HEADS - 2, TILE), jnp.float32),
        ],
        axis=0,
    )
    wide = pl.BlockSpec((TILE, Q_COLS), lambda j, c: (0, j))
    return pl.pallas_call(
        row_kernel,
        grid_spec=pltpu.PrefetchScalarGridSpec(
            num_scalar_prefetch=1,
            grid=(2,),
            in_specs=[
                wide,
                wide,
                pl.BlockSpec((MY_HEADS, TILE), lambda j, c: (j, 0)),
                pl.BlockSpec((SMALL_ROWS - 2 * MY_HEADS, TILE), lambda j, c: (0, 0)),
            ],
            out_specs=[pl.BlockSpec((SMALL_ROWS, TILE), lambda j, c: (0, 0))] * 2,
        ),
        out_shape=[jax.ShapeDtypeStruct((SMALL_ROWS, TILE), jnp.float32)] * 2,
        cost_estimate=pl.CostEstimate(
            flops=4 * 8 * TILE * QUERY_HEADS * HEAD_SIZE, bytes_accessed=2**21, transcendentals=0
        ),
    )(column[None].astype(jnp.int32), out, dout, lse, tail)


def add_back(arrived, part):
    if arrived.shape[0] < part.shape[0]:
        arrived = jnp.pad(arrived, ((0, part.shape[0] - arrived.shape[0]), (0, 0)))
    return (arrived.astype(jnp.float32) + part.astype(jnp.float32)).astype(jnp.bfloat16)


def shards(query, key, value, out, dout, lse, segment, bitmap):
    place = lax.axis_index(AXES)
    column = place % 2
    where = jnp.stack([column, place]).astype(jnp.int32)

    def half(array, side, size, axis):
        return lax.dynamic_slice_in_dim(array, side * size, size, axis)

    odd = segment % 2 == 1
    seg_code = jnp.where(odd, (segment + 1) // 2, 0)
    seg_row = jnp.tile(seg_code.astype(jnp.bfloat16)[None, :], (1, MY_KV))
    seg_block = jnp.broadcast_to(seg_row, (SEG_ROWS, KV_COLS))
    sent = jnp.concatenate(
        [half(key, 1 - column, KV_COLS, 1), half(value, 1 - column, KV_COLS, 1), seg_block], axis=0
    )
    came = swap(sent)
    mine = jnp.concatenate(
        [half(key, column, KV_COLS, 1), half(value, column, KV_COLS, 1), seg_block], axis=0
    )
    tile0 = jnp.where(column == 0, mine, came)
    tile1 = jnp.where(column == 0, came, mine)
    seg_both = jnp.concatenate(
        [tile1[2 * TILE : 2 * TILE + 1], tile0[2 * TILE : 2 * TILE + SEG_ROWS - 1]], axis=0
    )
    block = jnp.concatenate([tile1[: 2 * TILE], seg_both, tile0[: 2 * TILE]], axis=0)

    sent_q = jnp.concatenate(
        [half(query, 1 - column, Q_COLS, 1), half(dout, 1 - column, Q_COLS, 1)], axis=0
    )
    smalls = row_values(column, out, dout, lse, seg_code, bitmap)
    sm_own = smalls[0]
    sm_par = swap(smalls[1])
    sent_q, sm_par = lax.optimization_barrier((sent_q, sm_par))
    other = swap(sent_q)

    blocks = [block]
    parts = {}
    dq = None
    ahead = {5: 4, 6: 5, 7: 6, 8: 7}
    behind = {8: 3, 7: 2, 6: 1, 5: 0}
    for hop in range(1, HOPS + 1):
        going = blocks[-1]
        if hop == HOPS:
            going = going[:HALF_ROWS]
        blocks.append(shift(going, 2))
        if hop in ahead:
            s = ahead[hop]
            parts[s], dq = pair_grads((s,), *common, [blocks[s]], dq, False)
            blocks[-1], dq = lax.optimization_barrier((blocks[-1], dq))
        if hop == 1:
            blocks[-1], sm_par = lax.optimization_barrier((blocks[-1], sm_par))
        if hop == 4:
            turns = turned(column, query, dout, other, sm_own, sm_par)
            common = (where, query, dout, other, sm_own, sm_par, turns)
    total, dq = pair_grads((HOPS,), *common, [blocks[HOPS]], dq, False)
    dq_came = None
    for hop in range(HOPS, 0, -1):
        arrived = shift(total, -2)
        if hop in behind:
            s = behind[hop]
            if s > 0:
                parts[s], dq = pair_grads((s,), *common, [blocks[s]], dq, False)
                arrived, dq = lax.optimization_barrier((arrived, dq))
            else:
                parts[s], dq_own, dq_par = pair_grads((s,), *common, [blocks[s]], dq, True)
                arrived, dq_par = lax.optimization_barrier((arrived, dq_par))
                dq_came = swap(dq_par)
        total = add_back(arrived, parts[hop - 1])

    tile1, tile0 = total[: 2 * TILE], total[2 * TILE :]
    mine = jnp.where(column == 0, tile0, tile1)
    came = swap(jnp.where(column == 0, tile1, tile0))
    low = jnp.where(column == 0, mine, came)
    high = jnp.where(column == 0, came, mine)
    dkey = jnp.concatenate([low[:TILE], high[:TILE]], axis=1)
    dvalue = jnp.concatenate([low[TILE:], high[TILE:]], axis=1)
    dquery = jnp.concatenate(
        [jnp.where(column == 0, dq_own, dq_came), jnp.where(column == 0, dq_came, dq_own)], axis=1
    )
    return dquery, dkey, dvalue


def solution(mesh):
    rows = P(AXES, None)
    return jax.shard_map(
        shards,
        mesh=mesh,
        in_specs=(rows, rows, rows, rows, rows, P(None, AXES), P(AXES), P(AXES)),
        out_specs=(rows, rows, rows),
        check_vma=False,
    )
```

```python
import functools
import math

import jax
import jax.numpy as jnp
from jax import lax
from jax.experimental import pallas as pl
from jax.experimental.pallas import tpu as pltpu
from jax.sharding import PartitionSpec as P

QUERY_HEADS = 32
KEY_VALUE_HEADS = 4
HEAD_SIZE = 128
VISIBLE_TILES = 16
TILE = 128
GROUP = QUERY_HEADS // KEY_VALUE_HEADS

MY_HEADS = QUERY_HEADS // 2
MY_KV = KEY_VALUE_HEADS // 2
KV_COLS = MY_KV * HEAD_SIZE
Q_COLS = MY_HEADS * HEAD_SIZE
HOPS = VISIBLE_TILES // 2

SEG_ROWS = 16
K1, V1, SEG, K0, V0 = 0, TILE, 2 * TILE, 2 * TILE + SEG_ROWS, 3 * TILE + SEG_ROWS
HALF_ROWS = 2 * TILE + SEG_ROWS
FULL_ROWS = 4 * TILE + SEG_ROWS

SMALL_ROWS = 40
SCALE = HEAD_SIZE**-0.5
LOG2E = math.log2(math.e)
NEVER = -1e30
AXES = ("inner", "outer")


def shift(array, by):
    count = lax.axis_size(AXES)
    return lax.ppermute(array, AXES, [(i, (i + by) % count) for i in range(count)])


def swap(array):
    count = lax.axis_size(AXES)
    return lax.ppermute(array, AXES, [(i, i ^ 1) for i in range(count)])


def nt(a, b):
    return lax.dot_general(a, b, (((1,), (1,)), ((), ())), preferred_element_type=jnp.float32)


def nn(a, b):
    return jnp.dot(a, b, preferred_element_type=jnp.float32)


def turn_kernel(column_ref, q_own, do_own, q_par, sm_own, sm_par, q_turned, do_turned, columns):
    column = column_ref[0]

    @pl.loop(0, MY_KV)
    def _(kv):
        first = pl.multiple_of(kv * GROUP, GROUP)
        rows = []
        for at in (first, MY_HEADS + first):
            rows.append(
                jnp.concatenate([sm_own[pl.ds(at, GROUP), :], sm_par[pl.ds(at, GROUP), :]], axis=1)
            )
        rows.append(jnp.zeros((TILE - 2 * GROUP, 2 * TILE), jnp.float32))
        columns[kv] = jnp.concatenate(rows, axis=0).T
        for i in range(GROUP):
            head = first + i
            cols = pl.ds(pl.multiple_of(head * HEAD_SIZE, HEAD_SIZE), HEAD_SIZE)
            own_cols = pl.ds(
                pl.multiple_of((column * MY_HEADS + head) * HEAD_SIZE, HEAD_SIZE), HEAD_SIZE
            )
            at = slice(i * 2 * TILE, (i + 1) * 2 * TILE)
            q_turned[kv, :, at] = jnp.concatenate(
                [q_own[:, own_cols].T, q_par[0:TILE, cols].T], axis=1
            )
            do_turned[kv, :, at] = jnp.concatenate(
                [do_own[:, own_cols].T, q_par[TILE : 2 * TILE, cols].T], axis=1
            )


def turned(column, query, dout, other, sm_own, sm_par):
    here = pl.BlockSpec(memory_space=pltpu.VMEM)
    wide = jax.ShapeDtypeStruct((MY_KV, HEAD_SIZE, GROUP * 2 * TILE), jnp.bfloat16)
    return pl.pallas_call(
        turn_kernel,
        in_specs=[pl.BlockSpec(memory_space=pltpu.SMEM)] + [here] * 5,
        out_specs=[here] * 3,
        out_shape=[wide, wide, jax.ShapeDtypeStruct((MY_KV, 2 * TILE, TILE), jnp.float32)],
        compiler_params=pltpu.CompilerParams(vmem_limit_bytes=16 * 1024 * 1024),
        cost_estimate=pl.CostEstimate(flops=2**20, bytes_accessed=2**23, transcendentals=0),
    )(column[None].astype(jnp.int32), query, dout, other, sm_own, sm_par)


def pair_kernel(offsets, first, last, where_ref, *refs):
    count = len(offsets)
    q_own, q_par, do_own, sm_own, sm_par, q_turned, do_turned, columns = refs[:8]
    blocks = refs[8 : 8 + count]
    at = 8 + count
    dq_in = None
    if not first:
        dq_in = refs[at]
        at += 1
    parts = refs[at : at + count]
    at += count
    if last:
        dq_own, dq_par = refs[at : at + 2]
        at += 2
    else:
        dq_out = refs[at]
        at += 1
    biases = refs[at : at + count]
    column, place = where_ref[0], where_ref[1]

    row = lax.broadcasted_iota(jnp.int32, (TILE, TILE), 0)
    col = lax.broadcasted_iota(jnp.int32, (TILE, TILE), 1)
    for r, small in enumerate((sm_own, sm_par)):
        xq = column if r == 0 else 1 - column
        tile = place - column + xq
        words = small[2 * MY_HEADS + 1 : 2 * MY_HEADS + 2, :].astype(jnp.int32)
        q_seg = jnp.broadcast_to(small[2 * MY_HEADS : 2 * MY_HEADS + 1, :], (TILE, TILE)).T
        for n, s in enumerate(offsets):
            seg = blocks[n][SEG : SEG + SEG_ROWS, :TILE].astype(jnp.float32)
            for t in (1,) if s == HOPS else (0, 1):
                k_seg = jnp.broadcast_to(seg[1 - t : 2 - t, :], (TILE, TILE))
                w = 2 * s + xq - t
                bit = lax.shift_right_logical(words, jnp.broadcast_to(jnp.maximum(w, 0), words.shape)) & 1
                inside = (w >= 0) & (w < VISIBLE_TILES) & (tile - w >= 0)
                bit = jnp.where(w == 0, 1, bit)
                bit = jnp.where(inside, bit, 0)
                seen = (k_seg * q_seg * (k_seg - q_seg) == 0.0) & (
                    jnp.broadcast_to(bit, (TILE, TILE)) == 1
                )
                if s == 0:
                    seen = seen & ((row >= col) | (w != 0))
                k_at = 0 if s == HOPS else t * TILE
                biases[n][r * TILE : (r + 1) * TILE, k_at : k_at + TILE] = jnp.where(
                    seen, 0.0, NEVER
                )

    @pl.loop(0, MY_KV)
    def _(kv):
        kv_cols = pl.ds(pl.multiple_of(kv * HEAD_SIZE, HEAD_SIZE), HEAD_SIZE)
        loaded = []
        for n, s in enumerate(offsets):
            block = blocks[n]
            if s == HOPS:
                k, v = block[K1 : K1 + TILE, kv_cols], block[V1 : V1 + TILE, kv_cols]
            else:
                k = jnp.concatenate(
                    [block[K0 : K0 + TILE, kv_cols], block[K1 : K1 + TILE, kv_cols]], axis=0
                )
                v = jnp.concatenate(
                    [block[V0 : V0 + TILE, kv_cols], block[V1 : V1 + TILE, kv_cols]], axis=0
                )
            loaded.append((k, v, k.T, v.T))
        q_heads, do_heads = [], []
        for i in range(GROUP):
            head = kv * GROUP + i
            cols = pl.ds(pl.multiple_of(head * HEAD_SIZE, HEAD_SIZE), HEAD_SIZE)
            own_cols = pl.ds(
                pl.multiple_of((column * MY_HEADS + head) * HEAD_SIZE, HEAD_SIZE), HEAD_SIZE
            )
            q_heads += [q_own[:, own_cols], q_par[0:TILE, cols]]
            do_heads += [do_own[:, own_cols], q_par[TILE : 2 * TILE, cols]]
        q = jnp.concatenate(q_heads, axis=0)
        do = jnp.concatenate(do_heads, axis=0)
        totals = []
        dq = None
        for n in range(count):
            k, v, k_turned, v_turned = loaded[n]
            scores = nn(q, k_turned)
            dprob = nn(do, v_turned)
            probs, dscores = [], []
            for i in range(GROUP):
                at = slice(i * 2 * TILE, (i + 1) * 2 * TILE)
                neg_lse = columns[kv, :, i : i + 1]
                delta = columns[kv, :, GROUP + i : GROUP + i + 1]
                prob = jnp.exp2(scores[at] * (SCALE * LOG2E) + (biases[n][...] + neg_lse))
                probs.append(prob.astype(jnp.bfloat16))
                dscores.append((prob * (dprob[at] - delta)).astype(jnp.bfloat16))
            prob = jnp.concatenate(probs, axis=0)
            dscore = jnp.concatenate(dscores, axis=0)
            totals.append((nn(q_turned[kv], dscore), nn(do_turned[kv], prob)))
            more = nn(dscore, k)
            dq = more if dq is None else dq + more
        for i in range(GROUP):
            head = kv * GROUP + i
            cols = pl.ds(pl.multiple_of(head * HEAD_SIZE, HEAD_SIZE), HEAD_SIZE)
            part = dq[i * 2 * TILE : (i + 1) * 2 * TILE]
            if not first:
                part = part + dq_in[head]
            if last:
                part = (part * SCALE).astype(jnp.bfloat16)
                dq_own[:, cols] = part[:TILE]
                dq_par[:, cols] = part[TILE:]
            else:
                dq_out[head] = part
        for n, s in enumerate(offsets):
            dk_all = (totals[n][0] * SCALE).T.astype(jnp.bfloat16)
            dv_all = totals[n][1].T.astype(jnp.bfloat16)
            if s == HOPS:
                parts[n][0:TILE, kv_cols] = dk_all
                parts[n][TILE : 2 * TILE, kv_cols] = dv_all
            else:
                parts[n][0:TILE, kv_cols] = dk_all[TILE:]
                parts[n][TILE : 2 * TILE, kv_cols] = dv_all[TILE:]
                parts[n][2 * TILE : 3 * TILE, kv_cols] = dk_all[:TILE]
                parts[n][3 * TILE : 4 * TILE, kv_cols] = dv_all[:TILE]


def pair_grads(offsets, where, query, dout, other, sm_own, sm_par, turns, blocks, dq, last):
    first = dq is None
    keys = [TILE if s == HOPS else 2 * TILE for s in offsets]
    here = pl.BlockSpec(memory_space=pltpu.VMEM)
    args = [query, other, dout, sm_own, sm_par, *turns, *blocks]
    if not first:
        args.append(dq)
    out_shape = [jax.ShapeDtypeStruct((2 * k, KV_COLS), jnp.bfloat16) for k in keys]
    if last:
        out_shape += [jax.ShapeDtypeStruct((TILE, Q_COLS), jnp.bfloat16)] * 2
    else:
        out_shape.append(jax.ShapeDtypeStruct((MY_HEADS, 2 * TILE, HEAD_SIZE), jnp.float32))
    flops = sum(10 * MY_HEADS * k * 2 * TILE * HEAD_SIZE for k in keys)
    return pl.pallas_call(
        functools.partial(pair_kernel, offsets, first, last),
        in_specs=[pl.BlockSpec(memory_space=pltpu.SMEM)] + [here] * len(args),
        out_specs=[here] * len(out_shape),
        out_shape=out_shape,
        scratch_shapes=[pltpu.VMEM((2 * TILE, k), jnp.float32) for k in keys],
        input_output_aliases={} if first or last else {len(args): len(out_shape) - 1},
        compiler_params=pltpu.CompilerParams(vmem_limit_bytes=24 * 1024 * 1024),
        cost_estimate=pl.CostEstimate(
            flops=flops,
            bytes_accessed=8 * 1024 * 1024,
            transcendentals=sum(MY_HEADS * k * 2 * TILE for k in keys),
        ),
    )(where, *args)


def sum_up(*arrays):
    return sum(array.astype(jnp.float32) for array in arrays).astype(jnp.bfloat16)


def add_back(arrived, part):
    if part.shape[0] < arrived.shape[0]:
        part = jnp.pad(part, ((0, arrived.shape[0] - part.shape[0]), (0, 0)))
    return sum_up(arrived, part)


def row_kernel(column_ref, out_ref, dout_ref, lse_ref, tail_ref, own_ref, other_ref):
    step = pl.program_id(0)
    heads = QUERY_HEADS // 2
    ones = jnp.ones((8, HEAD_SIZE), jnp.bfloat16)
    rows = []
    for i in range(heads):
        cols = slice(i * HEAD_SIZE, (i + 1) * HEAD_SIZE)
        product = out_ref[:, cols].astype(jnp.float32) * dout_ref[:, cols].astype(jnp.float32)
        high = product.astype(jnp.bfloat16)
        low = (product - high.astype(jnp.float32)).astype(jnp.bfloat16)
        rows.append((nt(ones, high) + nt(ones, low))[:1])
    delta = jnp.concatenate(rows, axis=0)

    def fill(ref):
        ref[0:heads, :] = lse_ref[...] * (-LOG2E)
        ref[heads : 2 * heads, :] = delta
        ref[2 * heads : SMALL_ROWS, :] = tail_ref[...]

    @pl.when(step == column_ref[0])
    def _():
        fill(own_ref)

    @pl.when(step != column_ref[0])
    def _():
        fill(other_ref)


def row_values(column, out, dout, lse, seg_code, bitmap):
    tail = jnp.concatenate(
        [
            seg_code.astype(jnp.float32)[None, :],
            jnp.broadcast_to(bitmap.astype(jnp.float32)[None, :], (1, TILE)),
            jnp.zeros((SMALL_ROWS - 2 * MY_HEADS - 2, TILE), jnp.float32),
        ],
        axis=0,
    )
    wide = pl.BlockSpec((TILE, Q_COLS), lambda j, c: (0, j))
    return pl.pallas_call(
        row_kernel,
        grid_spec=pltpu.PrefetchScalarGridSpec(
            num_scalar_prefetch=1,
            grid=(2,),
            in_specs=[
                wide,
                wide,
                pl.BlockSpec((MY_HEADS, TILE), lambda j, c: (j, 0)),
                pl.BlockSpec((SMALL_ROWS - 2 * MY_HEADS, TILE), lambda j, c: (0, 0)),
            ],
            out_specs=[pl.BlockSpec((SMALL_ROWS, TILE), lambda j, c: (0, 0))] * 2,
        ),
        out_shape=[jax.ShapeDtypeStruct((SMALL_ROWS, TILE), jnp.float32)] * 2,
        cost_estimate=pl.CostEstimate(
            flops=4 * 8 * TILE * QUERY_HEADS * HEAD_SIZE, bytes_accessed=2**21, transcendentals=0
        ),
    )(column[None].astype(jnp.int32), out, dout, lse, tail)


def tie(first, second):
    return lax.optimization_barrier((first, second))


def shards(query, key, value, out, dout, lse, segment, bitmap):
    place = lax.axis_index(AXES)
    column = place % 2
    where = jnp.stack([column, place]).astype(jnp.int32)

    def half(array, side, size, axis):
        return lax.dynamic_slice_in_dim(array, side * size, size, axis)

    odd = segment % 2 == 1
    seg_code = jnp.where(odd, (segment + 1) // 2, 0)
    seg_row = jnp.tile(seg_code.astype(jnp.bfloat16)[None, :], (1, MY_KV))
    seg_block = jnp.broadcast_to(seg_row, (SEG_ROWS, KV_COLS))
    sent = jnp.concatenate(
        [half(key, 1 - column, KV_COLS, 1), half(value, 1 - column, KV_COLS, 1), seg_block], axis=0
    )
    lse, sent = tie(lse, sent)
    came = swap(sent)
    mine = jnp.concatenate(
        [half(key, column, KV_COLS, 1), half(value, column, KV_COLS, 1), seg_block], axis=0
    )
    tile0 = jnp.where(column == 0, mine, came)
    tile1 = jnp.where(column == 0, came, mine)
    seg_both = jnp.concatenate(
        [tile1[2 * TILE : 2 * TILE + 1], tile0[2 * TILE : 2 * TILE + SEG_ROWS - 1]], axis=0
    )
    block = jnp.concatenate([tile1[: 2 * TILE], seg_both, tile0[: 2 * TILE]], axis=0)

    sent_q = jnp.concatenate(
        [half(query, 1 - column, Q_COLS, 1), half(dout, 1 - column, Q_COLS, 1)], axis=0
    )
    smalls = row_values(column, out, dout, lse, seg_code, bitmap)
    sm_own = smalls[0]
    sm_par = swap(smalls[1])
    sent_q, sm_par = lax.optimization_barrier((sent_q, sm_par))
    other = swap(sent_q)

    blocks = {0: block}
    blocks[1] = shift(block, 2)
    far_block, sm_par = tie(block, sm_par)
    far_block, sent_q = tie(far_block, sent_q)
    blocks[8] = shift(far_block, 2 * HOPS)
    blocks[2] = shift(blocks[1], 2)

    parts = {}
    dq = None
    turns = turned(column, query, dout, other, sm_own, sm_par)

    def work(offsets, last=False):
        nonlocal dq
        common = (where, query, dout, other, sm_own, sm_par, turns)
        given = [blocks[s][:HALF_ROWS] if s == HOPS else blocks[s] for s in offsets]
        made = pair_grads(offsets, *common, given, dq, last)
        parts.update(zip(offsets, made))
        dq = made[len(offsets) :] if last else made[-1]

    def then(array):
        nonlocal dq
        array, dq = tie(array, dq)
        return array

    work((0, 1))
    blocks[8] = then(blocks[8])
    blocks[7] = shift(blocks[8], -2)
    blocks[2], blocks[8] = tie(blocks[2], blocks[8])
    blocks[3] = shift(blocks[2], 2)
    work((8,))
    work((2,))
    blocks[7] = then(blocks[7])
    blocks[3] = then(blocks[3])
    blocks[6] = shift(blocks[7], -2)
    blocks[4] = shift(blocks[3], 2)
    work((7,))
    work((3,))
    blocks[6] = then(blocks[6])
    blocks[4] = then(blocks[4])
    blocks[5] = shift(blocks[6], -2)
    work((6,))
    work((4,))
    near = shift(parts[4], -2)
    blocks[5] = then(blocks[5])
    work((5,), True)
    dq_own, dq_par = dq
    far = shift(parts[5], 2)
    near, dq_par = tie(near, dq_par)
    near = shift(add_back(near, parts[3]), -2)
    dq_came = swap(dq_par)
    far = shift(add_back(far, parts[6]), 2)
    near = shift(add_back(near, parts[2]), -2)
    far = shift(add_back(far, parts[7]), 2)
    far, near = tie(far, near)
    far = shift(add_back(far, parts[8]), -2 * HOPS)
    near = shift(add_back(near, parts[1]), -2)
    total = sum_up(near, parts[0], far)

    tile1, tile0 = total[: 2 * TILE], total[2 * TILE :]
    mine = jnp.where(column == 0, tile0, tile1)
    came = swap(jnp.where(column == 0, tile1, tile0))
    low = jnp.where(column == 0, mine, came)
    high = jnp.where(column == 0, came, mine)
    dkey = jnp.concatenate([low[:TILE], high[:TILE]], axis=1)
    dvalue = jnp.concatenate([low[TILE:], high[TILE:]], axis=1)
    dquery = jnp.concatenate(
        [jnp.where(column == 0, dq_own, dq_came), jnp.where(column == 0, dq_came, dq_own)], axis=1
    )
    return dquery, dkey, dvalue


def solution(mesh):
    rows = P(AXES, None)
    return jax.shard_map(
        shards,
        mesh=mesh,
        in_specs=(rows, rows, rows, rows, rows, P(None, AXES), P(AXES), P(AXES)),
        out_specs=(rows, rows, rows),
        check_vma=False,
    )
```

```python
import functools
import math

import jax
import jax.numpy as jnp
from jax import lax
from jax.experimental import pallas as pl
from jax.experimental.pallas import tpu as pltpu
from jax.sharding import PartitionSpec as P

QUERY_HEADS = 32
KEY_VALUE_HEADS = 4
HEAD_SIZE = 128
VISIBLE_TILES = 16
TILE = 128
GROUP = QUERY_HEADS // KEY_VALUE_HEADS

MY_HEADS = QUERY_HEADS // 2
MY_KV = KEY_VALUE_HEADS // 2
KV_COLS = MY_KV * HEAD_SIZE
Q_COLS = MY_HEADS * HEAD_SIZE
HOPS = VISIBLE_TILES // 2

SEG_ROWS = 16
K1, V1, SEG, K0, V0 = 0, TILE, 2 * TILE, 2 * TILE + SEG_ROWS, 3 * TILE + SEG_ROWS
HALF_ROWS = 2 * TILE + SEG_ROWS
FULL_ROWS = 4 * TILE + SEG_ROWS

SMALL_ROWS = 40
SCALE = HEAD_SIZE**-0.5
LOG2E = math.log2(math.e)
NEVER = -1e30
AXES = ("inner", "outer")


def shift(array, by):
    count = lax.axis_size(AXES)
    return lax.ppermute(array, AXES, [(i, (i + by) % count) for i in range(count)])


def swap(array):
    count = lax.axis_size(AXES)
    return lax.ppermute(array, AXES, [(i, i ^ 1) for i in range(count)])


def nt(a, b):
    return lax.dot_general(a, b, (((1,), (1,)), ((), ())), preferred_element_type=jnp.float32)


def nn(a, b):
    return jnp.dot(a, b, preferred_element_type=jnp.float32)


def turn_kernel(column_ref, q_own, do_own, q_par, sm_own, sm_par, q_turned, do_turned, columns):
    column = column_ref[0]

    @pl.loop(0, MY_KV)
    def _(kv):
        first = pl.multiple_of(kv * GROUP, GROUP)
        rows = []
        for at in (first, MY_HEADS + first):
            rows.append(
                jnp.concatenate([sm_own[pl.ds(at, GROUP), :], sm_par[pl.ds(at, GROUP), :]], axis=1)
            )
        rows.append(jnp.zeros((TILE - 2 * GROUP, 2 * TILE), jnp.float32))
        columns[kv] = jnp.concatenate(rows, axis=0).T
        for i in range(GROUP):
            head = first + i
            cols = pl.ds(pl.multiple_of(head * HEAD_SIZE, HEAD_SIZE), HEAD_SIZE)
            own_cols = pl.ds(
                pl.multiple_of((column * MY_HEADS + head) * HEAD_SIZE, HEAD_SIZE), HEAD_SIZE
            )
            at = slice(i * 2 * TILE, (i + 1) * 2 * TILE)
            q_turned[kv, :, at] = jnp.concatenate(
                [q_own[:, own_cols].T, q_par[0:TILE, cols].T], axis=1
            )
            do_turned[kv, :, at] = jnp.concatenate(
                [do_own[:, own_cols].T, q_par[TILE : 2 * TILE, cols].T], axis=1
            )


def turned(column, query, dout, other, sm_own, sm_par):
    here = pl.BlockSpec(memory_space=pltpu.VMEM)
    wide = jax.ShapeDtypeStruct((MY_KV, HEAD_SIZE, GROUP * 2 * TILE), jnp.bfloat16)
    return pl.pallas_call(
        turn_kernel,
        in_specs=[pl.BlockSpec(memory_space=pltpu.SMEM)] + [here] * 5,
        out_specs=[here] * 3,
        out_shape=[wide, wide, jax.ShapeDtypeStruct((MY_KV, 2 * TILE, TILE), jnp.float32)],
        compiler_params=pltpu.CompilerParams(vmem_limit_bytes=16 * 1024 * 1024),
        cost_estimate=pl.CostEstimate(flops=2**20, bytes_accessed=2**23, transcendentals=0),
    )(column[None].astype(jnp.int32), query, dout, other, sm_own, sm_par)


def pair_kernel(offsets, first, last, where_ref, *refs):
    count = len(offsets)
    q_own, q_par, do_own, sm_own, sm_par, q_turned, do_turned, columns = refs[:8]
    blocks = refs[8 : 8 + count]
    at = 8 + count
    dq_in = None
    if not first:
        dq_in = refs[at]
        at += 1
    parts = refs[at : at + count]
    at += count
    if last:
        dq_own, dq_par = refs[at : at + 2]
        at += 2
    else:
        dq_out = refs[at]
        at += 1
    biases = refs[at : at + count]
    column, place = where_ref[0], where_ref[1]

    row = lax.broadcasted_iota(jnp.int32, (TILE, TILE), 0)
    col = lax.broadcasted_iota(jnp.int32, (TILE, TILE), 1)
    for r, small in enumerate((sm_own, sm_par)):
        xq = column if r == 0 else 1 - column
        tile = place - column + xq
        words = small[2 * MY_HEADS + 1 : 2 * MY_HEADS + 2, :].astype(jnp.int32)
        q_seg = jnp.broadcast_to(small[2 * MY_HEADS : 2 * MY_HEADS + 1, :], (TILE, TILE)).T
        for n, s in enumerate(offsets):
            seg = blocks[n][SEG : SEG + SEG_ROWS, :TILE].astype(jnp.float32)
            for t in (1,) if s == HOPS else (0, 1):
                k_seg = jnp.broadcast_to(seg[1 - t : 2 - t, :], (TILE, TILE))
                w = 2 * s + xq - t
                bit = lax.shift_right_logical(words, jnp.broadcast_to(jnp.maximum(w, 0), words.shape)) & 1
                inside = (w >= 0) & (w < VISIBLE_TILES) & (tile - w >= 0)
                bit = jnp.where(w == 0, 1, bit)
                bit = jnp.where(inside, bit, 0)
                seen = (k_seg * q_seg * (k_seg - q_seg) == 0.0) & (
                    jnp.broadcast_to(bit, (TILE, TILE)) == 1
                )
                if s == 0:
                    seen = seen & ((row >= col) | (w != 0))
                k_at = 0 if s == HOPS else t * TILE
                biases[n][r * TILE : (r + 1) * TILE, k_at : k_at + TILE] = jnp.where(
                    seen, 0.0, NEVER
                )

    @pl.loop(0, MY_KV)
    def _(kv):
        kv_cols = pl.ds(pl.multiple_of(kv * HEAD_SIZE, HEAD_SIZE), HEAD_SIZE)
        loaded = []
        for n, s in enumerate(offsets):
            block = blocks[n]
            if s == HOPS:
                k, v = block[K1 : K1 + TILE, kv_cols], block[V1 : V1 + TILE, kv_cols]
            else:
                k = jnp.concatenate(
                    [block[K0 : K0 + TILE, kv_cols], block[K1 : K1 + TILE, kv_cols]], axis=0
                )
                v = jnp.concatenate(
                    [block[V0 : V0 + TILE, kv_cols], block[V1 : V1 + TILE, kv_cols]], axis=0
                )
            loaded.append((k, v, k.T, v.T))
        q_heads, do_heads = [], []
        for i in range(GROUP):
            head = kv * GROUP + i
            cols = pl.ds(pl.multiple_of(head * HEAD_SIZE, HEAD_SIZE), HEAD_SIZE)
            own_cols = pl.ds(
                pl.multiple_of((column * MY_HEADS + head) * HEAD_SIZE, HEAD_SIZE), HEAD_SIZE
            )
            q_heads += [q_own[:, own_cols], q_par[0:TILE, cols]]
            do_heads += [do_own[:, own_cols], q_par[TILE : 2 * TILE, cols]]
        q = jnp.concatenate(q_heads, axis=0)
        do = jnp.concatenate(do_heads, axis=0)
        totals = []
        dq = None
        for n in range(count):
            k, v, k_turned, v_turned = loaded[n]
            scores = nn(q, k_turned)
            dprob = nn(do, v_turned)
            probs, dscores = [], []
            for i in range(GROUP):
                at = slice(i * 2 * TILE, (i + 1) * 2 * TILE)
                neg_lse = columns[kv, :, i : i + 1]
                delta = columns[kv, :, GROUP + i : GROUP + i + 1]
                prob = jnp.exp2(scores[at] * (SCALE * LOG2E) + (biases[n][...] + neg_lse))
                probs.append(prob.astype(jnp.bfloat16))
                dscores.append((prob * (dprob[at] - delta)).astype(jnp.bfloat16))
            prob = jnp.concatenate(probs, axis=0)
            dscore = jnp.concatenate(dscores, axis=0)
            totals.append((nn(q_turned[kv], dscore), nn(do_turned[kv], prob)))
            more = nn(dscore, k)
            dq = more if dq is None else dq + more
        for i in range(GROUP):
            head = kv * GROUP + i
            cols = pl.ds(pl.multiple_of(head * HEAD_SIZE, HEAD_SIZE), HEAD_SIZE)
            part = dq[i * 2 * TILE : (i + 1) * 2 * TILE]
            if not first:
                part = part + dq_in[head]
            if last:
                part = (part * SCALE).astype(jnp.bfloat16)
                dq_own[:, cols] = part[:TILE]
                dq_par[:, cols] = part[TILE:]
            else:
                dq_out[head] = part
        for n, s in enumerate(offsets):
            dk_all = (totals[n][0] * SCALE).T.astype(jnp.bfloat16)
            dv_all = totals[n][1].T.astype(jnp.bfloat16)
            if s == HOPS:
                parts[n][0:TILE, kv_cols] = dk_all
                parts[n][TILE : 2 * TILE, kv_cols] = dv_all
            else:
                parts[n][0:TILE, kv_cols] = dk_all[TILE:]
                parts[n][TILE : 2 * TILE, kv_cols] = dv_all[TILE:]
                parts[n][2 * TILE : 3 * TILE, kv_cols] = dk_all[:TILE]
                parts[n][3 * TILE : 4 * TILE, kv_cols] = dv_all[:TILE]


def pair_grads(offsets, where, query, dout, other, sm_own, sm_par, turns, blocks, dq, last):
    first = dq is None
    keys = [TILE if s == HOPS else 2 * TILE for s in offsets]
    here = pl.BlockSpec(memory_space=pltpu.VMEM)
    args = [query, other, dout, sm_own, sm_par, *turns, *blocks]
    if not first:
        args.append(dq)
    out_shape = [jax.ShapeDtypeStruct((2 * k, KV_COLS), jnp.bfloat16) for k in keys]
    if last:
        out_shape += [jax.ShapeDtypeStruct((TILE, Q_COLS), jnp.bfloat16)] * 2
    else:
        out_shape.append(jax.ShapeDtypeStruct((MY_HEADS, 2 * TILE, HEAD_SIZE), jnp.float32))
    flops = sum(10 * MY_HEADS * k * 2 * TILE * HEAD_SIZE for k in keys)
    return pl.pallas_call(
        functools.partial(pair_kernel, offsets, first, last),
        in_specs=[pl.BlockSpec(memory_space=pltpu.SMEM)] + [here] * len(args),
        out_specs=[here] * len(out_shape),
        out_shape=out_shape,
        scratch_shapes=[pltpu.VMEM((2 * TILE, k), jnp.float32) for k in keys],
        input_output_aliases={} if first or last else {len(args): len(out_shape) - 1},
        compiler_params=pltpu.CompilerParams(vmem_limit_bytes=24 * 1024 * 1024),
        cost_estimate=pl.CostEstimate(
            flops=flops,
            bytes_accessed=8 * 1024 * 1024,
            transcendentals=sum(MY_HEADS * k * 2 * TILE for k in keys),
        ),
    )(where, *args)


def sum_up(*arrays):
    return sum(array.astype(jnp.float32) for array in arrays).astype(jnp.bfloat16)


def add_back(arrived, part):
    if part.shape[0] < arrived.shape[0]:
        part = jnp.pad(part, ((0, arrived.shape[0] - part.shape[0]), (0, 0)))
    return sum_up(arrived, part)


def row_kernel(column_ref, out_ref, dout_ref, lse_ref, tail_ref, own_ref, other_ref):
    step = pl.program_id(0)
    heads = QUERY_HEADS // 2
    ones = jnp.ones((8, HEAD_SIZE), jnp.bfloat16)
    rows = []
    for i in range(heads):
        cols = slice(i * HEAD_SIZE, (i + 1) * HEAD_SIZE)
        product = out_ref[:, cols].astype(jnp.float32) * dout_ref[:, cols].astype(jnp.float32)
        high = product.astype(jnp.bfloat16)
        low = (product - high.astype(jnp.float32)).astype(jnp.bfloat16)
        rows.append((nt(ones, high) + nt(ones, low))[:1])
    delta = jnp.concatenate(rows, axis=0)

    def fill(ref):
        ref[0:heads, :] = lse_ref[...] * (-LOG2E)
        ref[heads : 2 * heads, :] = delta
        ref[2 * heads : SMALL_ROWS, :] = tail_ref[...]

    @pl.when(step == column_ref[0])
    def _():
        fill(own_ref)

    @pl.when(step != column_ref[0])
    def _():
        fill(other_ref)


def row_values(column, out, dout, lse, seg_code, bitmap):
    tail = jnp.concatenate(
        [
            seg_code.astype(jnp.float32)[None, :],
            jnp.broadcast_to(bitmap.astype(jnp.float32)[None, :], (1, TILE)),
            jnp.zeros((SMALL_ROWS - 2 * MY_HEADS - 2, TILE), jnp.float32),
        ],
        axis=0,
    )
    wide = pl.BlockSpec((TILE, Q_COLS), lambda j, c: (0, j))
    return pl.pallas_call(
        row_kernel,
        grid_spec=pltpu.PrefetchScalarGridSpec(
            num_scalar_prefetch=1,
            grid=(2,),
            in_specs=[
                wide,
                wide,
                pl.BlockSpec((MY_HEADS, TILE), lambda j, c: (j, 0)),
                pl.BlockSpec((SMALL_ROWS - 2 * MY_HEADS, TILE), lambda j, c: (0, 0)),
            ],
            out_specs=[pl.BlockSpec((SMALL_ROWS, TILE), lambda j, c: (0, 0))] * 2,
        ),
        out_shape=[jax.ShapeDtypeStruct((SMALL_ROWS, TILE), jnp.float32)] * 2,
        cost_estimate=pl.CostEstimate(
            flops=4 * 8 * TILE * QUERY_HEADS * HEAD_SIZE, bytes_accessed=2**21, transcendentals=0
        ),
    )(column[None].astype(jnp.int32), out, dout, lse, tail)


def tie(first, second):
    return lax.optimization_barrier((first, second))


def shards(query, key, value, out, dout, lse, segment, bitmap):
    place = lax.axis_index(AXES)
    column = place % 2
    where = jnp.stack([column, place]).astype(jnp.int32)

    def half(array, side, size, axis):
        return lax.dynamic_slice_in_dim(array, side * size, size, axis)

    odd = segment % 2 == 1
    seg_code = jnp.where(odd, (segment + 1) // 2, 0)
    seg_row = jnp.tile(seg_code.astype(jnp.bfloat16)[None, :], (1, MY_KV))
    seg_block = jnp.broadcast_to(seg_row, (SEG_ROWS, KV_COLS))
    sent = jnp.concatenate(
        [half(key, 1 - column, KV_COLS, 1), half(value, 1 - column, KV_COLS, 1), seg_block], axis=0
    )
    lse, sent = tie(lse, sent)
    came = swap(sent)
    mine = jnp.concatenate(
        [half(key, column, KV_COLS, 1), half(value, column, KV_COLS, 1), seg_block], axis=0
    )
    tile0 = jnp.where(column == 0, mine, came)
    tile1 = jnp.where(column == 0, came, mine)
    seg_both = jnp.concatenate(
        [tile1[2 * TILE : 2 * TILE + 1], tile0[2 * TILE : 2 * TILE + SEG_ROWS - 1]], axis=0
    )
    block = jnp.concatenate([tile1[: 2 * TILE], seg_both, tile0[: 2 * TILE]], axis=0)

    sent_q = jnp.concatenate(
        [half(query, 1 - column, Q_COLS, 1), half(dout, 1 - column, Q_COLS, 1)], axis=0
    )
    smalls = row_values(column, out, dout, lse, seg_code, bitmap)
    sm_own = smalls[0]
    sm_par = swap(smalls[1])
    sent_q, sm_par = lax.optimization_barrier((sent_q, sm_par))
    other = swap(sent_q)

    blocks = {0: block}
    blocks[1] = shift(block, 2)
    far_block, sm_par = tie(block, sm_par)
    far_block, sent_q = tie(far_block, sent_q)
    blocks[8] = shift(far_block, 2 * HOPS)
    blocks[2] = shift(blocks[1], 2)

    parts = {}
    dq = None
    turns = turned(column, query, dout, other, sm_own, sm_par)

    def work(offsets, last=False):
        nonlocal dq
        common = (where, query, dout, other, sm_own, sm_par, turns)
        given = [blocks[s][:HALF_ROWS] if s == HOPS else blocks[s] for s in offsets]
        made = pair_grads(offsets, *common, given, dq, last)
        parts.update(zip(offsets, made))
        dq = made[len(offsets) :] if last else made[-1]

    def then(array):
        nonlocal dq
        array, dq = tie(array, dq)
        return array

    work((0, 1))
    blocks[8] = then(blocks[8])
    blocks[7] = shift(blocks[8], -2)
    blocks[2], blocks[8] = tie(blocks[2], blocks[8])
    blocks[3] = shift(blocks[2], 2)
    work((8, 2))
    blocks[7] = then(blocks[7])
    blocks[3] = then(blocks[3])
    blocks[6] = shift(blocks[7], -2)
    blocks[4] = shift(blocks[3], 2)
    work((7, 3))
    blocks[6] = then(blocks[6])
    blocks[4] = then(blocks[4])
    blocks[5] = shift(blocks[6], -2)
    work((6, 4))
    near = shift(parts[4], -2)
    blocks[5] = then(blocks[5])
    work((5,), True)
    dq_own, dq_par = dq
    far = shift(parts[5], 2)
    near, dq_par = tie(near, dq_par)
    near = shift(add_back(near, parts[3]), -2)
    dq_came = swap(dq_par)
    far = shift(add_back(far, parts[6]), 2)
    near = shift(add_back(near, parts[2]), -2)
    far = shift(add_back(far, parts[7]), 2)
    far, near = tie(far, near)
    far = shift(add_back(far, parts[8]), -2 * HOPS)
    near = shift(add_back(near, parts[1]), -2)
    total = sum_up(near, parts[0], far)

    tile1, tile0 = total[: 2 * TILE], total[2 * TILE :]
    mine = jnp.where(column == 0, tile0, tile1)
    came = swap(jnp.where(column == 0, tile1, tile0))
    low = jnp.where(column == 0, mine, came)
    high = jnp.where(column == 0, came, mine)
    dkey = jnp.concatenate([low[:TILE], high[:TILE]], axis=1)
    dvalue = jnp.concatenate([low[TILE:], high[TILE:]], axis=1)
    dquery = jnp.concatenate(
        [jnp.where(column == 0, dq_own, dq_came), jnp.where(column == 0, dq_came, dq_own)], axis=1
    )
    return dquery, dkey, dvalue


def solution(mesh):
    rows = P(AXES, None)
    return jax.shard_map(
        shards,
        mesh=mesh,
        in_specs=(rows, rows, rows, rows, rows, P(None, AXES), P(AXES), P(AXES)),
        out_specs=(rows, rows, rows),
        check_vma=False,
    )
```

```python
import functools
import math

import jax
import jax.numpy as jnp
from jax import lax
from jax.experimental import pallas as pl
from jax.experimental.pallas import tpu as pltpu
from jax.sharding import PartitionSpec as P

QUERY_HEADS = 32
KEY_VALUE_HEADS = 4
HEAD_SIZE = 128
VISIBLE_TILES = 16
TILE = 128
GROUP = QUERY_HEADS // KEY_VALUE_HEADS

MY_HEADS = QUERY_HEADS // 2
MY_KV = KEY_VALUE_HEADS // 2
KV_COLS = MY_KV * HEAD_SIZE
Q_COLS = MY_HEADS * HEAD_SIZE
HOPS = VISIBLE_TILES // 2

SEG_ROWS = 16
K1, V1, SEG, K0, V0 = 0, TILE, 2 * TILE, 2 * TILE + SEG_ROWS, 3 * TILE + SEG_ROWS
HALF_ROWS = 2 * TILE + SEG_ROWS
FULL_ROWS = 4 * TILE + SEG_ROWS

SMALL_ROWS = 40
SCALE = HEAD_SIZE**-0.5
LOG2E = math.log2(math.e)
NEVER = -1e30
AXES = ("inner", "outer")


def shift(array, by):
    count = lax.axis_size(AXES)
    return lax.ppermute(array, AXES, [(i, (i + by) % count) for i in range(count)])


def swap(array):
    count = lax.axis_size(AXES)
    return lax.ppermute(array, AXES, [(i, i ^ 1) for i in range(count)])


def nt(a, b):
    return lax.dot_general(a, b, (((1,), (1,)), ((), ())), preferred_element_type=jnp.float32)


def nn(a, b):
    return jnp.dot(a, b, preferred_element_type=jnp.float32)


def turn_kernel(column_ref, q_own, do_own, q_par, sm_own, sm_par, q_turned, do_turned, columns):
    column = column_ref[0]

    @pl.loop(0, MY_KV)
    def _(kv):
        first = pl.multiple_of(kv * GROUP, GROUP)
        rows = []
        for at in (first, MY_HEADS + first):
            rows.append(
                jnp.concatenate([sm_own[pl.ds(at, GROUP), :], sm_par[pl.ds(at, GROUP), :]], axis=1)
            )
        rows.append(jnp.zeros((TILE - 2 * GROUP, 2 * TILE), jnp.float32))
        columns[kv] = jnp.concatenate(rows, axis=0).T
        for i in range(GROUP):
            head = first + i
            cols = pl.ds(pl.multiple_of(head * HEAD_SIZE, HEAD_SIZE), HEAD_SIZE)
            own_cols = pl.ds(
                pl.multiple_of((column * MY_HEADS + head) * HEAD_SIZE, HEAD_SIZE), HEAD_SIZE
            )
            at = slice(i * 2 * TILE, (i + 1) * 2 * TILE)
            q_turned[kv, :, at] = jnp.concatenate(
                [q_own[:, own_cols].T, q_par[0:TILE, cols].T], axis=1
            )
            do_turned[kv, :, at] = jnp.concatenate(
                [do_own[:, own_cols].T, q_par[TILE : 2 * TILE, cols].T], axis=1
            )


def turned(column, query, dout, other, sm_own, sm_par):
    here = pl.BlockSpec(memory_space=pltpu.VMEM)
    wide = jax.ShapeDtypeStruct((MY_KV, HEAD_SIZE, GROUP * 2 * TILE), jnp.bfloat16)
    return pl.pallas_call(
        turn_kernel,
        in_specs=[pl.BlockSpec(memory_space=pltpu.SMEM)] + [here] * 5,
        out_specs=[here] * 3,
        out_shape=[wide, wide, jax.ShapeDtypeStruct((MY_KV, 2 * TILE, TILE), jnp.float32)],
        compiler_params=pltpu.CompilerParams(vmem_limit_bytes=16 * 1024 * 1024),
        cost_estimate=pl.CostEstimate(flops=2**20, bytes_accessed=2**23, transcendentals=0),
    )(column[None].astype(jnp.int32), query, dout, other, sm_own, sm_par)


def pair_kernel(offsets, first, last, where_ref, *refs):
    count = len(offsets)
    q_own, q_par, do_own, sm_own, sm_par, q_turned, do_turned, columns = refs[:8]
    blocks = refs[8 : 8 + count]
    at = 8 + count
    dq_in = None
    if not first:
        dq_in = refs[at]
        at += 1
    parts = refs[at : at + count]
    at += count
    if last:
        dq_own, dq_par = refs[at : at + 2]
        at += 2
    else:
        dq_out = refs[at]
        at += 1
    biases = refs[at : at + count]
    column, place = where_ref[0], where_ref[1]

    row = lax.broadcasted_iota(jnp.int32, (TILE, TILE), 0)
    col = lax.broadcasted_iota(jnp.int32, (TILE, TILE), 1)
    for r, small in enumerate((sm_own, sm_par)):
        xq = column if r == 0 else 1 - column
        tile = place - column + xq
        words = small[2 * MY_HEADS + 1 : 2 * MY_HEADS + 2, :].astype(jnp.int32)
        q_seg = jnp.broadcast_to(small[2 * MY_HEADS : 2 * MY_HEADS + 1, :], (TILE, TILE)).T
        for n, s in enumerate(offsets):
            seg = blocks[n][SEG : SEG + SEG_ROWS, :TILE].astype(jnp.float32)
            for t in (1,) if s == HOPS else (0, 1):
                k_seg = jnp.broadcast_to(seg[1 - t : 2 - t, :], (TILE, TILE))
                w = 2 * s + xq - t
                bit = lax.shift_right_logical(words, jnp.broadcast_to(jnp.maximum(w, 0), words.shape)) & 1
                inside = (w >= 0) & (w < VISIBLE_TILES) & (tile - w >= 0)
                bit = jnp.where(w == 0, 1, bit)
                bit = jnp.where(inside, bit, 0)
                seen = (k_seg * q_seg * (k_seg - q_seg) == 0.0) & (
                    jnp.broadcast_to(bit, (TILE, TILE)) == 1
                )
                if s == 0:
                    seen = seen & ((row >= col) | (w != 0))
                k_at = 0 if s == HOPS else t * TILE
                biases[n][r * TILE : (r + 1) * TILE, k_at : k_at + TILE] = jnp.where(
                    seen, 0.0, NEVER
                )

    @pl.loop(0, MY_KV)
    def _(kv):
        kv_cols = pl.ds(pl.multiple_of(kv * HEAD_SIZE, HEAD_SIZE), HEAD_SIZE)
        loaded = []
        for n, s in enumerate(offsets):
            block = blocks[n]
            if s == HOPS:
                k, v = block[K1 : K1 + TILE, kv_cols], block[V1 : V1 + TILE, kv_cols]
            else:
                k = jnp.concatenate(
                    [block[K0 : K0 + TILE, kv_cols], block[K1 : K1 + TILE, kv_cols]], axis=0
                )
                v = jnp.concatenate(
                    [block[V0 : V0 + TILE, kv_cols], block[V1 : V1 + TILE, kv_cols]], axis=0
                )
            loaded.append((k, v, k.T, v.T))
        q_heads, do_heads = [], []
        for i in range(GROUP):
            head = kv * GROUP + i
            cols = pl.ds(pl.multiple_of(head * HEAD_SIZE, HEAD_SIZE), HEAD_SIZE)
            own_cols = pl.ds(
                pl.multiple_of((column * MY_HEADS + head) * HEAD_SIZE, HEAD_SIZE), HEAD_SIZE
            )
            q_heads += [q_own[:, own_cols], q_par[0:TILE, cols]]
            do_heads += [do_own[:, own_cols], q_par[TILE : 2 * TILE, cols]]
        q = jnp.concatenate(q_heads, axis=0)
        do = jnp.concatenate(do_heads, axis=0)
        totals = []
        dq = None
        for n in range(count):
            k, v, k_turned, v_turned = loaded[n]
            scores = nn(q, k_turned)
            dprob = nn(do, v_turned)
            probs, dscores = [], []
            for i in range(GROUP):
                at = slice(i * 2 * TILE, (i + 1) * 2 * TILE)
                neg_lse = columns[kv, :, i : i + 1]
                delta = columns[kv, :, GROUP + i : GROUP + i + 1]
                prob = jnp.exp2(scores[at] * (SCALE * LOG2E) + (biases[n][...] + neg_lse))
                probs.append(prob.astype(jnp.bfloat16))
                dscores.append((prob * (dprob[at] - delta)).astype(jnp.bfloat16))
            prob = jnp.concatenate(probs, axis=0)
            dscore = jnp.concatenate(dscores, axis=0)
            totals.append((nn(q_turned[kv], dscore), nn(do_turned[kv], prob)))
            more = nn(dscore, k)
            dq = more if dq is None else dq + more
        for i in range(GROUP):
            head = kv * GROUP + i
            cols = pl.ds(pl.multiple_of(head * HEAD_SIZE, HEAD_SIZE), HEAD_SIZE)
            part = dq[i * 2 * TILE : (i + 1) * 2 * TILE]
            if not first:
                part = part + dq_in[head]
            if last:
                part = (part * SCALE).astype(jnp.bfloat16)
                dq_own[:, cols] = part[:TILE]
                dq_par[:, cols] = part[TILE:]
            else:
                dq_out[head] = part
        for n, s in enumerate(offsets):
            dk_all = (totals[n][0] * SCALE).T.astype(jnp.bfloat16)
            dv_all = totals[n][1].T.astype(jnp.bfloat16)
            if s == HOPS:
                parts[n][0:TILE, kv_cols] = dk_all
                parts[n][TILE : 2 * TILE, kv_cols] = dv_all
            else:
                parts[n][0:TILE, kv_cols] = dk_all[TILE:]
                parts[n][TILE : 2 * TILE, kv_cols] = dv_all[TILE:]
                parts[n][2 * TILE : 3 * TILE, kv_cols] = dk_all[:TILE]
                parts[n][3 * TILE : 4 * TILE, kv_cols] = dv_all[:TILE]


def pair_grads(offsets, where, query, dout, other, sm_own, sm_par, turns, blocks, dq, last):
    first = dq is None
    keys = [TILE if s == HOPS else 2 * TILE for s in offsets]
    here = pl.BlockSpec(memory_space=pltpu.VMEM)
    args = [query, other, dout, sm_own, sm_par, *turns, *blocks]
    if not first:
        args.append(dq)
    out_shape = [jax.ShapeDtypeStruct((2 * k, KV_COLS), jnp.bfloat16) for k in keys]
    if last:
        out_shape += [jax.ShapeDtypeStruct((TILE, Q_COLS), jnp.bfloat16)] * 2
    else:
        out_shape.append(jax.ShapeDtypeStruct((MY_HEADS, 2 * TILE, HEAD_SIZE), jnp.float32))
    flops = sum(10 * MY_HEADS * k * 2 * TILE * HEAD_SIZE for k in keys)
    return pl.pallas_call(
        functools.partial(pair_kernel, offsets, first, last),
        in_specs=[pl.BlockSpec(memory_space=pltpu.SMEM)] + [here] * len(args),
        out_specs=[here] * len(out_shape),
        out_shape=out_shape,
        scratch_shapes=[pltpu.VMEM((2 * TILE, k), jnp.float32) for k in keys],
        input_output_aliases={} if first or last else {len(args): len(out_shape) - 1},
        compiler_params=pltpu.CompilerParams(vmem_limit_bytes=24 * 1024 * 1024),
        cost_estimate=pl.CostEstimate(
            flops=flops,
            bytes_accessed=8 * 1024 * 1024,
            transcendentals=sum(MY_HEADS * k * 2 * TILE for k in keys),
        ),
    )(where, *args)


def sum_up(*arrays):
    return sum(array.astype(jnp.float32) for array in arrays).astype(jnp.bfloat16)


def add_back(arrived, part):
    if part.shape[0] < arrived.shape[0]:
        part = jnp.pad(part, ((0, arrived.shape[0] - part.shape[0]), (0, 0)))
    return sum_up(arrived, part)


def row_kernel(column_ref, bitmap_ref, out_ref, dout_ref, lse_ref, segment_ref, own_ref, other_ref):
    heads = MY_HEADS
    ones = jnp.ones((8, HEAD_SIZE), jnp.bfloat16)
    segment = segment_ref[...]
    seg_code = jnp.where(segment & 1 == 1, (segment + 1) >> 1, 0).astype(jnp.float32)
    words = jnp.full((1, TILE), bitmap_ref[0], jnp.int32).astype(jnp.float32)
    empty = jnp.zeros((SMALL_ROWS - 2 * heads - 2, TILE), jnp.float32)
    for side in range(2):
        rows = []
        for i in range(side * heads, (side + 1) * heads):
            cols = slice(i * HEAD_SIZE, (i + 1) * HEAD_SIZE)
            product = out_ref[:, cols].astype(jnp.float32) * dout_ref[:, cols].astype(jnp.float32)
            high = product.astype(jnp.bfloat16)
            low = (product - high.astype(jnp.float32)).astype(jnp.bfloat16)
            rows.append((nt(ones, high) + nt(ones, low))[:1])
        neg_lse = lse_ref[side * heads : (side + 1) * heads, :] * (-LOG2E)
        filled = jnp.concatenate([neg_lse, *rows, seg_code, words, empty], axis=0)

        @pl.when(column_ref[0] == side)
        def _():
            own_ref[...] = filled

        @pl.when(column_ref[0] != side)
        def _():
            other_ref[...] = filled


def row_values(column, out, dout, lse, segment, bitmap):
    here = pl.BlockSpec(memory_space=pltpu.VMEM)
    return pl.pallas_call(
        row_kernel,
        in_specs=[pl.BlockSpec(memory_space=pltpu.SMEM)] * 2 + [here] * 4,
        out_specs=[here] * 2,
        out_shape=[jax.ShapeDtypeStruct((SMALL_ROWS, TILE), jnp.float32)] * 2,
        compiler_params=pltpu.CompilerParams(vmem_limit_bytes=16 * 1024 * 1024),
        cost_estimate=pl.CostEstimate(
            flops=4 * 8 * TILE * QUERY_HEADS * HEAD_SIZE, bytes_accessed=2**21, transcendentals=0
        ),
    )(column[None].astype(jnp.int32), bitmap, out, dout, lse, segment[None, :])


def tie(first, second):
    return lax.optimization_barrier((first, second))


def shards(query, key, value, out, dout, lse, segment, bitmap):
    place = lax.axis_index(AXES)
    column = place % 2
    where = jnp.stack([column, place]).astype(jnp.int32)

    def half(array, side, size, axis):
        return lax.dynamic_slice_in_dim(array, side * size, size, axis)

    odd = segment % 2 == 1
    seg_code = jnp.where(odd, (segment + 1) // 2, 0)
    seg_row = jnp.tile(seg_code.astype(jnp.bfloat16)[None, :], (1, MY_KV))
    seg_block = jnp.broadcast_to(seg_row, (SEG_ROWS, KV_COLS))
    sent = jnp.concatenate(
        [half(key, 1 - column, KV_COLS, 1), half(value, 1 - column, KV_COLS, 1), seg_block], axis=0
    )
    lse, sent = tie(lse, sent)
    came = swap(sent)
    mine = jnp.concatenate(
        [half(key, column, KV_COLS, 1), half(value, column, KV_COLS, 1), seg_block], axis=0
    )
    tile0 = jnp.where(column == 0, mine, came)
    tile1 = jnp.where(column == 0, came, mine)
    seg_both = jnp.concatenate(
        [tile1[2 * TILE : 2 * TILE + 1], tile0[2 * TILE : 2 * TILE + SEG_ROWS - 1]], axis=0
    )
    block = jnp.concatenate([tile1[: 2 * TILE], seg_both, tile0[: 2 * TILE]], axis=0)

    sent_q = jnp.concatenate(
        [half(query, 1 - column, Q_COLS, 1), half(dout, 1 - column, Q_COLS, 1)], axis=0
    )
    smalls = row_values(column, out, dout, lse, segment, bitmap)
    sm_own = smalls[0]
    sm_par = swap(smalls[1])
    sent_q, sm_par = lax.optimization_barrier((sent_q, sm_par))
    other = swap(sent_q)

    blocks = {0: block}
    blocks[1] = shift(block, 2)
    far_block, sm_par = tie(block, sm_par)
    far_block, sent_q = tie(far_block, sent_q)
    blocks[8] = shift(far_block, 2 * HOPS)
    blocks[2] = shift(blocks[1], 2)

    parts = {}
    dq = None
    turns = turned(column, query, dout, other, sm_own, sm_par)

    def work(offsets, last=False):
        nonlocal dq
        common = (where, query, dout, other, sm_own, sm_par, turns)
        given = [blocks[s][:HALF_ROWS] if s == HOPS else blocks[s] for s in offsets]
        made = pair_grads(offsets, *common, given, dq, last)
        parts.update(zip(offsets, made))
        dq = made[len(offsets) :] if last else made[-1]

    def then(array):
        nonlocal dq
        array, dq = tie(array, dq)
        return array

    work((0, 1))
    blocks[8] = then(blocks[8])
    blocks[7] = shift(blocks[8], -2)
    blocks[2], blocks[8] = tie(blocks[2], blocks[8])
    blocks[3] = shift(blocks[2], 2)
    work((8, 2))
    blocks[7] = then(blocks[7])
    blocks[3] = then(blocks[3])
    blocks[6] = shift(blocks[7], -2)
    blocks[4] = shift(blocks[3], 2)
    work((7, 3))
    blocks[6] = then(blocks[6])
    blocks[4] = then(blocks[4])
    blocks[5] = shift(blocks[6], -2)
    work((6, 4))
    near = shift(parts[4], -2)
    blocks[5] = then(blocks[5])
    work((5,), True)
    dq_own, dq_par = dq
    far = shift(parts[5], 2)
    near, dq_par = tie(near, dq_par)
    near = shift(add_back(near, parts[3]), -2)
    dq_came = swap(dq_par)
    far = shift(add_back(far, parts[6]), 2)
    near = shift(add_back(near, parts[2]), -2)
    far = shift(add_back(far, parts[7]), 2)
    far, near = tie(far, near)
    far = shift(add_back(far, parts[8]), -2 * HOPS)
    near = shift(add_back(near, parts[1]), -2)
    total = sum_up(near, parts[0], far)

    tile1, tile0 = total[: 2 * TILE], total[2 * TILE :]
    mine = jnp.where(column == 0, tile0, tile1)
    came = swap(jnp.where(column == 0, tile1, tile0))
    low = jnp.where(column == 0, mine, came)
    high = jnp.where(column == 0, came, mine)
    dkey = jnp.concatenate([low[:TILE], high[:TILE]], axis=1)
    dvalue = jnp.concatenate([low[TILE:], high[TILE:]], axis=1)
    dquery = jnp.concatenate(
        [jnp.where(column == 0, dq_own, dq_came), jnp.where(column == 0, dq_came, dq_own)], axis=1
    )
    return dquery, dkey, dvalue


def solution(mesh):
    rows = P(AXES, None)
    return jax.shard_map(
        shards,
        mesh=mesh,
        in_specs=(rows, rows, rows, rows, rows, P(None, AXES), P(AXES), P(AXES)),
        out_specs=(rows, rows, rows),
        check_vma=False,
    )
```
